32 devices in a mesh: gx: 8 (over z, y), gz: 4 (over x, core).
Axes of the slice: x: 2, y: 2, z: 4, core: 2. Of those that a mesh axis runs over, the one named last changes fastest.
Arguments:
- thermal_undercool: float32 [16, 384, 512], P(None, 'gx', 'gz'), may hold values from -1 to 1
- mixture_alloying: float32 [16, 384, 512], P(None, 'gx', 'gz'), may hold values from 0.5 to 1.5
- fluid_fraction: float32 [16, 384, 512], P(None, 'gx', 'gz'), may hold values from 0.05 to 0.95
- kozeny_factor: float32 [16, 384, 512], P(None, 'gx', 'gz'), may hold values from 0.5 to 2
- state_marker: int32 [16, 384, 512], P(None, 'gx', 'gz'), may hold values from 0 to 2
Outputs:
- pressure: float32 [16, 384, 512], P(None, 'gx', 'gz')
- solute_out: float32 [16, 384, 512], P(None, 'gx', 'gz')
The draws below stay inside these ranges and needn't reach their ends.
Inputs may be any that keep to these rules, and one draw needn't show every extreme that they name: `state_marker`: 0 marks a mushy cell, 1 a liquid one, 2 a solid one.
All inputs are finite; a program needn't handle non-finite values.
Results may differ from the reference program's by a relative error of at most 0.0003.
Values sent between devices are 32-bit elements; how exact they have to be, the bound alone decides.
A program may use at most 64 MiB of HBM per device.

```python
import math
import jax
import jax.numpy as jnp

SLAB_LAYER_COUNT = 16
STEPS = 4
SWEEPS = 3
MESH_WIDTH_COUNT = 384
MESH_DEPTH_COUNT = 512


def place_ends(array, key, smallest, high):
    index_at = [jax.random.randint(jax.random.fold_in(key, axis), (), 0, length) for axis, length in enumerate(array.shape)]
    widest = array.shape.index(max(array.shape))
    neighbour = index_at[:widest] + [(index_at[widest] + 1) % array.shape[widest]] + index_at[widest + 1:]
    return array.at[tuple(index_at)].set(smallest).at[tuple(neighbour)].set(high)


def block_levels(key, shape, split, smallest, high):
    gain, own = 1.0, jax.random.fold_in(key, 6)
    for dim, shards_of in split:
        draws = jnp.exp(jax.random.uniform(jax.random.fold_in(own, dim), (shards_of,), jnp.float32, smallest / len(split), high / len(split)))
        gain = gain * jnp.repeat(draws, shape[dim] // shards_of).reshape([-1 if axis == dim else 1 for axis in range(len(shape))])
    return gain


def setup_inputs(seed: int = 0) -> dict:
    key_list = jax.random.split(jax.random.key(seed), 6)
    thermal_undercool = jnp.clip(jax.random.uniform(key_list[0], (SLAB_LAYER_COUNT, MESH_WIDTH_COUNT, MESH_DEPTH_COUNT), jnp.float32, -1.0, 1.0) * block_levels(key_list[0], (SLAB_LAYER_COUNT, MESH_WIDTH_COUNT, MESH_DEPTH_COUNT), ((1, 8), (2, 4)), -0.4, 0.0), -1.0, 1.0)
    mixture_alloying = jnp.clip(0.5 + 1.0 * jax.random.uniform(key_list[1], (SLAB_LAYER_COUNT, MESH_WIDTH_COUNT, MESH_DEPTH_COUNT), jnp.float32) ** block_levels(key_list[1], (SLAB_LAYER_COUNT, MESH_WIDTH_COUNT, MESH_DEPTH_COUNT), ((1, 8), (2, 4)), -0.2, 0.2), 0.5, 1.5)
    fluid_fraction = jnp.clip(0.05 + 0.9 * jax.random.uniform(key_list[2], (SLAB_LAYER_COUNT, MESH_WIDTH_COUNT, MESH_DEPTH_COUNT), jnp.float32) ** block_levels(key_list[2], (SLAB_LAYER_COUNT, MESH_WIDTH_COUNT, MESH_DEPTH_COUNT), ((1, 8), (2, 4)), -0.2, 0.2), 0.05, 0.95)
    kozeny_factor = jnp.clip(jnp.exp(math.log(2.0) - 1.3862944 * jax.random.uniform(key_list[3], (SLAB_LAYER_COUNT, MESH_WIDTH_COUNT, MESH_DEPTH_COUNT), jnp.float32) ** block_levels(key_list[3], (SLAB_LAYER_COUNT, MESH_WIDTH_COUNT, MESH_DEPTH_COUNT), ((1, 8), (2, 4)), -0.2, 0.2)), 0.5, 2.0)
    state_marker = place_ends(jax.random.randint(key_list[4], (SLAB_LAYER_COUNT, MESH_WIDTH_COUNT, MESH_DEPTH_COUNT), 0, 3), jax.random.fold_in(key_list[4], 1), 0, 2).astype(jnp.int32)
    return dict(thermal_undercool=thermal_undercool, mixture_alloying=mixture_alloying, fluid_fraction=fluid_fraction, kozeny_factor=kozeny_factor, state_marker=state_marker)


solute_rate = 0.5


def zero_rim(field):
    return jnp.pad(field, ((0, 0), (1, 1), (1, 1)))


def neighbours_of(extended):
    center = extended[:, 1:-1, 1:-1]
    padded = jnp.pad(center, ((1, 1), (0, 0), (0, 0)))
    return center, [extended[:, 2:, 1:-1], extended[:, :-2, 1:-1], padded[2:], padded[:-2], extended[:, 1:-1, 2:], extended[:, 1:-1, :-2]]


def face_terms(perm_ext, density_ext, gravity):
    perm_mid, perm_near = neighbours_of(perm_ext)
    density_mid, density_near = neighbours_of(density_ext)
    conductance = [0.5 * (perm_mid + other) for other in perm_near]
    diagonal = conductance[0]
    for face_index in range(1, 6):
        diagonal = diagonal + conductance[face_index]
    lift_down = gravity * 0.5 * (density_mid + density_near[4])
    lift_up = -(gravity * 0.5 * (density_mid + density_near[5]))
    return conductance, diagonal, lift_down, lift_up


def jacobi_sweep(pressure_ext, coupling, forcing_amount):
    conductance, diagonal, lift_down, lift_up = coupling
    _, pressure_near = neighbours_of(pressure_ext)
    numerator = forcing_amount - conductance[4] * lift_down - conductance[5] * lift_up
    for face_index in range(6):
        numerator = numerator + conductance[face_index] * pressure_near[face_index]
    return numerator / diagonal


def solute_update(pressure_ext, conc_ext, coupling, molten_state):
    conductance, _, lift_down, lift_up = coupling
    pressure_mid, pressure_near = neighbours_of(pressure_ext)
    conc_mid, conc_near = neighbours_of(conc_ext)
    change = jnp.zeros_like(conc_mid)
    for face_index in range(6):
        driving = pressure_mid - pressure_near[face_index]
        if face_index == 4:
            driving = driving + lift_down
        if face_index == 5:
            driving = driving + lift_up
        flow_out = conductance[face_index] * driving
        change = change + jnp.maximum(flow_out, 0.0) * conc_mid + jnp.minimum(flow_out, 0.0) * conc_near[face_index]
    return conc_mid - solute_rate * change / (molten_state + 0.1)


def reference(thermal_undercool, mixture_alloying, fluid_fraction, kozeny_factor, state_marker):
    gravity = 4.0 / MESH_DEPTH_COUNT
    molten_state = jnp.where(state_marker == 1, 1.0, jnp.where(state_marker == 2, 0.0, fluid_fraction)).astype(jnp.float32)
    darcian_conductivity = kozeny_factor * (molten_state ** 3 / ((1.0 - molten_state) ** 2 + 0.25) + 0.02)
    forcing_amount = 2.0 * molten_state * (1.0 - molten_state) * thermal_undercool
    perm_ext = zero_rim(darcian_conductivity)
    alloying_content = mixture_alloying
    pressure = jnp.zeros_like(mixture_alloying)
    for time_step in range(STEPS):
        molten_mass_per_volume = 1.0 + 0.2 * alloying_content - 0.3 * thermal_undercool
        metal_head = gravity * (jnp.cumsum(molten_mass_per_volume, axis=2) - 0.5 * molten_mass_per_volume)
        coupling = face_terms(perm_ext, zero_rim(molten_mass_per_volume), gravity)
        pressure = metal_head
        for sweep_index in range(SWEEPS):
            pressure = jacobi_sweep(zero_rim(pressure), coupling, forcing_amount)
        alloying_content = solute_update(zero_rim(pressure), zero_rim(alloying_content), coupling, molten_state)
    return pressure, alloying_content
```

```python
import functools

import jax
import jax.numpy as jnp
from jax import lax
from jax.experimental import pallas as pl
from jax.experimental.pallas import tpu as pltpu
from jax.sharding import PartitionSpec as P

STEPS = 4
SWEEPS = 3
W = SWEEPS + 1
SOLUTE_RATE = 0.5
MESH = pl.DeviceIdType.MESH
UNROLL = 2

LO = 8


def kernel(nx, nz, *refs):
    it = iter(refs)
    t_in, c_in, f_in, k_in, m_in, p_out, c_out = [next(it) for _ in range(7)]
    perm, temp, ca, cb, pa, pb = [next(it) for _ in range(6)]
    axp, axm, ayp, aym, azp, azm, srcn = [next(it) for _ in range(7)]
    cxp, cyp, czp, czm, rl, bb, ld, lu = [next(it) for _ in range(8)]
    hf = next(it)
    off = next(it)
    xs, xr, rs, rr, es, er, ls, lr, fs, fr = [next(it) for _ in range(10)]
    sxs, sxr, szs, szr, ses, ser = [next(it) for _ in range(6)]
    send_sem, recv_sem, st_send, st_recv = [next(it) for _ in range(4)]

    ny, n, lanes = t_in.shape
    wide = n + 2 * W
    hi_row = LO + wide
    mid = LO + W
    gravity = 4.0 / (nz * lanes)
    half = 0.5 * gravity
    ix, iz = lax.axis_index("gx"), lax.axis_index("gz")
    f32, bf16 = jnp.float32, jnp.bfloat16

    CONC, PERM, TEMP, SRC, PH, BH, AXP, AXM, AYP, AYM, AZP, AZM, SRCN, RHO = range(14)

    def inside(dx, dz):
        return (ix + dx >= 0) & (ix + dx < nx) & (iz + dz >= 0) & (iz + dz < nz)

    partners = [(dx, dz) for dz in range(-1, nz) for dx in (-1, 0, 1) if (dx, dz) != (0, 0)]

    def step_copies(s):
        out = []
        for dx, dz in partners:
            a, b = (1, 0) if dx > 0 else (0, 1)
            if dz == 0:
                src, dst = xs.at[s, a], xr.at[s, b]
            elif dz > 0 and dx == 0:
                src, dst = rs.at[s], rr.at[s, dz - 1]
            elif dz > 0:
                src, dst = es.at[s, a], er.at[s, b, dz - 1]
            elif dx == 0:
                src, dst = ls.at[s], lr.at[s]
            else:
                src, dst = fs.at[s, a], fr.at[s, b]
            m = len(out)
            out.append((dx, dz, pltpu.make_async_remote_copy(
                src_ref=src, dst_ref=dst, send_sem=send_sem.at[s, m], recv_sem=recv_sem.at[s, m],
                device_id={"gx": ix + dx, "gz": iz + dz}, device_id_type=MESH)))
        return out

    def static_copies():
        out = []
        for dx, dz in partners:
            if dz > 1:
                continue
            a, b = (1, 0) if dx > 0 else (0, 1)
            if dz == 0:
                src, dst = sxs.at[a], sxr.at[b]
            elif dx == 0:
                src, dst = szs, szr.at[0 if dz > 0 else 1]
            else:
                src, dst = ses.at[a], ser.at[b, 0 if dz > 0 else 1]
            m = len(out)
            out.append((dx, dz, pltpu.make_async_remote_copy(
                src_ref=src, dst_ref=dst, send_sem=st_send.at[m], recv_sem=st_recv.at[m],
                device_id={"gx": ix + dx, "gz": iz + dz}, device_id_type=MESH)))
        return out

    def start(copies):
        for dx, dz, c in copies:
            pl.when(inside(dx, dz))(c.start)

    def arrive(copies):
        for dx, dz, c in copies:
            pl.when(inside(-dx, -dz))(c.wait_recv)

    def sent(copies):
        for dx, dz, c in copies:
            pl.when(inside(dx, dz))(c.wait_send)

    for ref in (xr, rr, er, lr, fr, sxr, szr, ser):
        ref[...] = jnp.zeros_like(ref)
    barrier = pltpu.get_barrier_semaphore()
    count = 0
    for dx, dz in partners:
        @pl.when(inside(-dx, -dz))
        def _(dx=dx, dz=dz):
            pl.semaphore_signal(barrier, inc=1, device_id={"gx": ix - dx, "gz": iz - dz}, device_id_type=MESH)
        count = count + inside(dx, dz).astype(jnp.int32)

    def yloop(body, init):
        def group(g, carry):
            for u in range(UNROLL):
                carry = body(g * UNROLL + u, carry)
            return carry
        return lax.fori_loop(0, ny // UNROLL, group, init)

    lane_n = lax.broadcasted_iota(jnp.int32, (n, lanes), 1)
    lane_w = lax.broadcasted_iota(jnp.int32, (wide, lanes), 1)
    per = lanes // ny

    def lane(rows):
        return lane_n if rows == n else lane_w

    def fold(acc, value, y, roll=True):
        moved = pltpu.roll(value, y * per + W, 1) if roll else value
        return jnp.where(lane(value.shape[0]) // per == y, moved, acc)

    def z_near(value, packed, y):
        e = pltpu.roll(packed, lanes - W - y * per, 1)
        ln = lane(value.shape[0])
        up = pltpu.roll(jnp.where(ln == lanes - 1, e, value), 1, 1)
        down = pltpu.roll(jnp.where(ln == 0, e, value), lanes - 1, 1)
        return down, up

    k_w = lane_w % per

    def z_near_packed(packed, own):
        up = pltpu.roll(jnp.where(k_w == W - 1, own, packed), 1, 1)
        down = pltpu.roll(jnp.where(k_w == W, own, packed), lanes - 1, 1)
        return down, up

    def y_near_packed(packed):
        return pltpu.roll(packed, lanes - per, 1), pltpu.roll(packed, per, 1)

    def split_dot(value, weights):
        high = value.astype(bf16)
        low = (value - high.astype(f32)).astype(bf16)
        return jnp.dot(jnp.concatenate([high, low], axis=1), weights, preferred_element_type=f32)

    r2 = lax.broadcasted_iota(jnp.int32, (2 * lanes, lanes), 0) % lanes
    c2 = lax.broadcasted_iota(jnp.int32, (2 * lanes, lanes), 1)
    ones = jnp.ones((2 * lanes, lanes), bf16)
    before = jnp.where(r2 < c2, 1.0, jnp.where(r2 == c2, 0.5, 0.0)).astype(bf16)
    both = jnp.concatenate([before, ones], axis=1)
    kr, kc = r2 % per, c2 % per
    same = (r2 // per) == (c2 // per)
    after_w = jnp.where(kr == kc, 0.5, jnp.where((kr >= W) & (kr < kc), 1.0, 0.0))
    before_w = jnp.where(kr == kc, -0.5, jnp.where((kr < W) & (kr > kc), -1.0, 0.0))
    packed_sum = jnp.where(same, jnp.where(kc >= W, after_w, before_w), 0.0).astype(bf16)

    zslab = jnp.zeros(perm.shape[1:], f32)
    for ref in (perm, ca, cb, pa, pb):
        ref[0] = zslab
        ref[ny + 1] = zslab
    zrows = jnp.zeros((LO, lanes), f32)

    def clear(y, carry):
        for ref in (perm, pa, pb, ca, cb):
            ref[y + 1, 0:LO, :] = zrows
            ref[y + 1, hi_row:hi_row + LO, :] = zrows
        return carry
    yloop(clear, 0)
    cyp[0] = zslab
    cxp[:, 0:LO, :] = jnp.zeros((ny, LO, lanes), f32)
    hf[...] = jnp.zeros_like(hf)

    zn = jnp.zeros((n, lanes), f32)
    center = pl.ds(mid, n)
    window = pl.ds(LO, wide)

    def own_fields(y, carry):
        zp, zt, zs, zc, tot = carry
        mark, t, c = m_in[y], t_in[y], c_in[y]
        liq = jnp.where(mark == 1, 1.0, jnp.where(mark == 2, 0.0, f_in[y]))
        solid = 1.0 - liq
        pm = k_in[y] * (liq * liq * liq / (solid * solid + 0.25) + 0.02)
        sr = 2.0 * liq * solid * t
        perm[y + 1, center, :] = pm
        temp[y, center, :] = t
        srcn[y, center, :] = sr
        ca[y + 1, center, :] = c
        rl[y] = SOLUTE_RATE / (liq + 0.1)
        for f, v in enumerate((pm, t, sr)):
            sxs[0, f, y] = v[0:W]
            sxs[1, f, y] = v[n - W:n]
        xs[0, 0, y] = c[0:W]
        xs[0, 1, y] = c[n - W:n]
        tot_y = split_dot(1.0 + 0.2 * c - 0.3 * t, ones)
        return (fold(zp, pm, y), fold(zt, t, y), fold(zs, sr, y), fold(zc, c, y), fold(tot, tot_y, y, False))

    def post(s, zc, tot):
        r = jnp.where(lane_n % per < W, zc, tot)
        rs[s] = r
        ls[s] = zc
        es[s, 0] = r[0:W]
        es[s, 1] = r[n - W:n]
        fs[s, 0] = zc[0:W]
        fs[s, 1] = zc[n - W:n]
        start(step_copies(s))

    zp, zt, zs, zc, tot = yloop(own_fields, (zn,) * 5)
    for f, v in enumerate((zp, zt, zs)):
        szs[f] = v
        ses[0, f] = v[0:W]
        ses[1, f] = v[n - W:n]
    pl.semaphore_wait(barrier, count)
    start(static_copies())
    post(0, zc, tot)

    top, bottom = pl.ds(LO, W), pl.ds(mid + n, W)
    k_n = lane_n % per
    k_e = lax.broadcasted_iota(jnp.int32, (W, lanes), 1) % per

    arrive(static_copies())
    for f, h in enumerate((PERM, TEMP, SRC)):
        hf[h, center, :] = jnp.where(k_n < W, szr[0, f], szr[1, f])
        hf[h, top, :] = jnp.where(k_e < W, ser[0, 0, f], ser[0, 1, f])
        hf[h, bottom, :] = jnp.where(k_e < W, ser[1, 0, f], ser[1, 1, f])

    def spread(y, carry):
        for f, (ref, o) in enumerate(((perm, 1), (temp, 0), (srcn, 0))):
            ref[y + o, top, :] = sxr[0, f, y]
            ref[y + o, bottom, :] = sxr[1, f, y]
        return carry
    yloop(spread, 0)

    up_rows, down_rows = pl.ds(LO + 1, wide), pl.ds(LO - 1, wide)

    def diagonal_of(pm, near):
        c = [0.5 * (pm + other) for other in near]
        total = c[0] + c[1] + c[2] + c[3] + c[4] + c[5]
        inv = jnp.where(pm > 0.0, 1.0 / jnp.where(pm > 0.0, total, 1.0), 0.0)
        return c, inv

    def coefficients(y, acc):
        pm = perm[y + 1, window, :]
        dz, uz = z_near(pm, hf[PERM, window, :], y)
        c, inv = diagonal_of(pm, [perm[y + 1, up_rows, :], perm[y + 1, down_rows, :],
                                  perm[y + 2, window, :], perm[y, window, :], dz, uz])
        cxp[y, window, :] = c[0]
        cyp[y + 1, window, :] = c[2]

        @pl.when(y == 0)
        def _():
            cyp[0, window, :] = c[3]
        czp[y, window, :] = c[4]
        czm[y, window, :] = c[5]
        for ref, v in zip((axp, axm, ayp, aym, azp, azm), c):
            ref[y] = v * inv
        srcn[y, window, :] = srcn[y, window, :] * inv
        return fold(acc, pm, y)

    zw = jnp.zeros((wide, lanes), f32)
    own = yloop(coefficients, zw)
    pm = hf[PERM, window, :]
    yp, ym = y_near_packed(pm)
    first, last = lane_w < per, lane_w >= lanes - per
    yp, ym = jnp.where(last, 0.0, yp), jnp.where(first, 0.0, ym)
    dz, uz = z_near_packed(pm, own)
    c, inv = diagonal_of(pm, [hf[PERM, up_rows, :], hf[PERM, down_rows, :], yp, ym, dz, uz])
    c[2], c[3] = jnp.where(last, 0.0, c[2]), jnp.where(first, 0.0, c[3])
    for h, v in zip((AXP, AXM, AYP, AYM, AZP, AZM, SRCN), c + [hf[SRC, window, :]]):
        hf[h, window, :] = v * inv

    conc, conc_next = ca, cb
    for s in range(STEPS):
        arrive(step_copies(s))
        hf[CONC, center, :] = jnp.where(k_n < W, rr[s, 0], lr[s])
        hf[CONC, top, :] = jnp.where(k_e < W, er[s, 0, 0], fr[s, 0])
        hf[CONC, bottom, :] = jnp.where(k_e < W, er[s, 1, 0], fr[s, 1])
        total = [rr[s, 0], er[s, 0, 0], er[s, 1, 0]]
        for d in range(1, nz - 1):
            total = [total[0] + rr[s, d], total[1] + er[s, 0, d], total[2] + er[s, 1, d]]
        off[center, :], off[top, :], off[bottom, :] = total
        hpm = hf[PERM, window, :]
        hrho = jnp.where(hpm > 0.0, 1.0 + 0.2 * hf[CONC, window, :] - 0.3 * hf[TEMP, window, :], 0.0)
        hf[RHO, window, :] = hrho

        def head(y, carry, conc=conc, s=s):
            acc, tot = carry
            conc[y + 1, top, :] = xr[s, 0, y]
            conc[y + 1, bottom, :] = xr[s, 1, y]
            real = perm[y + 1, window, :] > 0.0
            rho = jnp.where(real, 1.0 + 0.2 * conc[y + 1, window, :] - 0.3 * temp[y, window, :], 0.0)
            sums = split_dot(rho, both)
            above = pltpu.roll(off[window, :], lanes - W - y * per, 1)[:, 0:1]
            pa[y + 1, window, :] = jnp.where(real, gravity * (above + sums[:, 0:lanes]), 0.0)
            dz, uz = z_near(rho, hf[RHO, window, :], y)
            down, up = half * (rho + dz), half * (rho + uz)
            ld[y, window, :] = down
            lu[y, window, :] = up
            bb[y] = srcn[y, window, :] - azp[y] * down + azm[y] * up
            return fold(acc, rho, y), fold(tot, sums[:, lanes:2 * lanes], y, False)

        own, tot = yloop(head, (zw, zw))
        above = off[window, :]
        above = jnp.where(k_w >= W, above + tot, pltpu.roll(above, lanes - W, 1))
        hf[PH, window, :] = jnp.where(hpm > 0.0, gravity * (above + split_dot(hrho, packed_sum)), 0.0)
        dz, uz = z_near_packed(hrho, own)
        hf[BH, window, :] = hf[SRCN, window, :] - half * (
            hf[AZP, window, :] * (hrho + dz) - hf[AZM, window, :] * (hrho + uz))

        old, new = pa, pb
        for sweep in range(SWEEPS):
            def relax(y, acc, old=old, new=new):
                p = old[y + 1, window, :]
                dz, uz = z_near(p, hf[PH, window, :], y)
                v = bb[y] + axp[y] * old[y + 1, up_rows, :] + axm[y] * old[y + 1, down_rows, :]
                v = v + (ayp[y] * old[y + 2, window, :] + aym[y] * old[y, window, :])
                v = v + (azp[y] * dz + azm[y] * uz)
                new[y + 1, window, :] = v
                return fold(acc, p, y)

            own = yloop(relax, zw)
            p = hf[PH, window, :]
            dz, uz = z_near_packed(p, own)
            yp, ym = y_near_packed(p)
            v = hf[BH, window, :] + hf[AXP, window, :] * hf[PH, up_rows, :] + hf[AXM, window, :] * hf[PH, down_rows, :]
            v = v + hf[AYP, window, :] * yp + hf[AYM, window, :] * ym
            v = v + hf[AZP, window, :] * dz + hf[AZM, window, :] * uz
            hf[PH, window, :] = v
            old, new = new, old

        final = s == STEPS - 1
        up_c, down_c = pl.ds(mid + 1, n), pl.ds(mid - 1, n)

        def transport(y, carry, old=old, conc=conc, conc_next=conc_next, s=s, final=final):
            p, c = old[y + 1, center, :], conc[y + 1, center, :]
            pdz, puz = z_near(p, hf[PH, center, :], y)
            cdz, cuz = z_near(c, hf[CONC, center, :], y)

            def carried(flow, near):
                return flow * jnp.where(flow > 0.0, c, near)

            change = carried(cxp[y, center, :] * (p - old[y + 1, up_c, :]), conc[y + 1, up_c, :])
            change = change + carried(cxp[y, down_c, :] * (p - old[y + 1, down_c, :]), conc[y + 1, down_c, :])
            change = change + carried(cyp[y + 1, center, :] * (p - old[y + 2, center, :]), conc[y + 2, center, :])
            change = change + carried(cyp[y, center, :] * (p - old[y, center, :]), conc[y, center, :])
            change = change + carried(czp[y, center, :] * (p - pdz + ld[y, center, :]), cdz)
            change = change + carried(czm[y, center, :] * (p - puz - lu[y, center, :]), cuz)
            fresh = c - rl[y] * change
            if final:
                p_out[y] = p
                c_out[y] = fresh
                return carry
            zc, tot = carry
            conc_next[y + 1, center, :] = fresh
            xs[s + 1, 0, y] = fresh[0:W]
            xs[s + 1, 1, y] = fresh[n - W:n]
            tot_y = split_dot(1.0 + 0.2 * fresh - 0.3 * t_in[y], ones)
            return fold(zc, fresh, y), fold(tot, tot_y, y, False)

        if final:
            yloop(transport, 0)
        else:
            zc, tot = yloop(transport, (zn, zn))
            post(s + 1, zc, tot)
        conc, conc_next = conc_next, conc

    sent(static_copies())
    for s in range(STEPS):
        sent(step_copies(s))


def on_device(nx, nz, *args):
    ny, n, lanes = args[0].shape
    wide = n + 2 * W
    rows = wide + 2 * LO
    partners = 3 * (nz + 1) - 1

    def vmem(*shape):
        return pltpu.VMEM(shape, jnp.float32)

    padded, layered = (ny + 2, rows, lanes), (ny, rows, lanes)
    scratch = [vmem(*padded), vmem(*layered)] + [vmem(*padded)] * 4
    scratch += [vmem(ny, wide, lanes)] * 6 + [vmem(*layered)]
    scratch += [vmem(*layered), vmem(ny + 1, rows, lanes), vmem(*layered), vmem(*layered),
                vmem(ny, n, lanes), vmem(ny, wide, lanes), vmem(*layered), vmem(*layered)]
    scratch += [vmem(14, rows, lanes), vmem(rows, lanes)]
    scratch += [vmem(STEPS, 2, ny, W, lanes)] * 2
    scratch += [vmem(STEPS, n, lanes), vmem(STEPS, nz - 1, n, lanes)]
    scratch += [vmem(STEPS, 2, W, lanes), vmem(STEPS, 2, nz - 1, W, lanes)]
    scratch += [vmem(STEPS, n, lanes)] * 2 + [vmem(STEPS, 2, W, lanes)] * 2
    scratch += [vmem(2, 3, ny, W, lanes)] * 2
    scratch += [vmem(3, n, lanes), vmem(2, 3, n, lanes), vmem(2, 3, W, lanes), vmem(2, 2, 3, W, lanes)]
    scratch += [pltpu.SemaphoreType.DMA((STEPS, partners))] * 2 + [pltpu.SemaphoreType.DMA((8,))] * 2
    return tuple(pl.pallas_call(
        functools.partial(kernel, nx, nz),
        out_shape=[jax.ShapeDtypeStruct((ny, n, lanes), jnp.float32)] * 2,
        in_specs=[pl.BlockSpec(memory_space=pltpu.VMEM)] * 5,
        out_specs=[pl.BlockSpec(memory_space=pltpu.VMEM)] * 2,
        scratch_shapes=scratch,
        compiler_params=pltpu.CompilerParams(
            collective_id=0, has_side_effects=True, vmem_limit_bytes=40 * 1024 * 1024),
    )(*args))


def solution(mesh):
    placed = P(None, "gx", "gz")
    return jax.shard_map(
        functools.partial(on_device, mesh.shape["gx"], mesh.shape["gz"]),
        mesh=mesh,
        in_specs=(placed,) * 5,
        out_specs=(placed, placed),
        check_vma=False,
    )
```

```python
import functools

import jax
import jax.numpy as jnp
from jax import lax
from jax.experimental import pallas as pl
from jax.experimental.pallas import tpu as pltpu
from jax.sharding import PartitionSpec as P

STEPS = 4
SWEEPS = 3
W = SWEEPS + 1
SOLUTE_RATE = 0.5
MESH = pl.DeviceIdType.MESH
UNROLL = 4

LO = 8


def kernel(nx, nz, *refs):
    it = iter(refs)
    hbm = [next(it) for _ in range(5)]
    p_out, c_out = [next(it) for _ in range(2)]
    t_in, c_in, f_in, k_in, m_in = staged = [next(it) for _ in range(5)]
    perm, temp, ca, cb, pa, pb = [next(it) for _ in range(6)]
    axp, axm, ayp, aym, azp, azm, srcn = [next(it) for _ in range(7)]
    cxp, cyp, czp, czm, rl, bb, ld, lu = [next(it) for _ in range(8)]
    hf = next(it)
    off, totp, hl, pf, hx, hxt = [next(it) for _ in range(6)]
    xs, xr, zs, zr, es, er, ts, tr = [next(it) for _ in range(8)]
    sxs, sxr, szs, szr, ses, ser = [next(it) for _ in range(6)]
    send_sem, recv_sem, st_send, st_recv, in_sem = [next(it) for _ in range(5)]

    ny, n, lanes = t_in.shape
    wide = n + 2 * W
    hi_row = LO + wide
    mid = LO + W
    gravity = 4.0 / (nz * lanes)
    half = 0.5 * gravity
    ix, iz = lax.axis_index("gx"), lax.axis_index("gz")
    f32, bf16 = jnp.float32, jnp.bfloat16

    CONC, PERM, TEMP, SRC, PH, BH, AXP, AXM, AYP, AYM, AZP, AZM, SRCN, RHO = range(14)

    def inside(dx, dz):
        return (ix + dx >= 0) & (ix + dx < nx) & (iz + dz >= 0) & (iz + dz < nz)

    partners = [(dx, dz) for dz in range(-1, nz) for dx in (-1, 0, 1) if (dx, dz) != (0, 0)]

    def step_copies(s, totals):
        plan = []
        for dx, dz in partners:
            a, b = (1, 0) if dx > 0 else (0, 1)
            if dz == 0:
                plan.append((dx, dz, xs.at[s, a], xr.at[s, b]))
            elif dz in (-1, 1) and dx == 0:
                plan.append((dx, dz, zs.at[s], zr.at[s, 0 if dz > 0 else 1]))
            elif dz in (-1, 1):
                plan.append((dx, dz, es.at[s, a], er.at[s, b, 0 if dz > 0 else 1]))
            if dz > 0:
                plan.append((dx, dz, ts.at[s], tr.at[s, 1 - dx, dz - 1]))
        return [(dx, dz, pltpu.make_async_remote_copy(
            src_ref=src, dst_ref=dst, send_sem=send_sem.at[s, m], recv_sem=recv_sem.at[s, m],
            device_id={"gx": ix + dx, "gz": iz + dz}, device_id_type=MESH))
            for m, (dx, dz, src, dst) in enumerate(plan) if (dst.shape == (8, lanes)) == totals]

    def static_copies():
        out = []
        for dx, dz in partners:
            if dz > 1:
                continue
            a, b = (1, 0) if dx > 0 else (0, 1)
            if dz == 0:
                src, dst = sxs.at[a], sxr.at[b]
            elif dx == 0:
                src, dst = szs, szr.at[0 if dz > 0 else 1]
            else:
                src, dst = ses.at[a], ser.at[b, 0 if dz > 0 else 1]
            m = len(out)
            out.append((dx, dz, pltpu.make_async_remote_copy(
                src_ref=src, dst_ref=dst, send_sem=st_send.at[m], recv_sem=st_recv.at[m],
                device_id={"gx": ix + dx, "gz": iz + dz}, device_id_type=MESH)))
        return out

    def start(copies):
        for dx, dz, c in copies:
            pl.when(inside(dx, dz))(c.start)

    def arrive(copies):
        for dx, dz, c in copies:
            pl.when(inside(-dx, -dz))(c.wait_recv)

    def sent(copies):
        for dx, dz, c in copies:
            pl.when(inside(dx, dz))(c.wait_send)

    loads = [pltpu.make_async_copy(a, b, in_sem.at[i]) for i, (a, b) in enumerate(zip(hbm, staged))]
    for load in loads:
        load.start()

    for ref in (xr, zr, er, tr, sxr, szr, ser):
        ref[...] = jnp.zeros_like(ref)
    barrier = pltpu.get_barrier_semaphore()
    count = 0
    for dx, dz in partners:
        @pl.when(inside(-dx, -dz))
        def _(dx=dx, dz=dz):
            pl.semaphore_signal(barrier, inc=1, device_id={"gx": ix - dx, "gz": iz - dz}, device_id_type=MESH)
        count = count + inside(dx, dz).astype(jnp.int32)

    def yloop(body, init):
        def group(g, carry):
            for u in range(UNROLL):
                carry = body(g * UNROLL + u, carry)
            return carry
        return lax.fori_loop(0, ny // UNROLL, group, init)

    lane_n = lax.broadcasted_iota(jnp.int32, (n, lanes), 1)
    lane_w = lax.broadcasted_iota(jnp.int32, (wide, lanes), 1)
    per = lanes // ny

    def lane(rows):
        return lane_n if rows == n else lane_w

    def fold(acc, value, y, roll=True):
        moved = pltpu.roll(value, y * per + W, 1) if roll else value
        return jnp.where(lane(value.shape[0]) // per == y, moved, acc)

    def z_near(value, packed, y):
        e = pltpu.roll(packed, lanes - W - y * per, 1)
        ln = lane(value.shape[0])
        up = pltpu.roll(jnp.where(ln == lanes - 1, e, value), 1, 1)
        down = pltpu.roll(jnp.where(ln == 0, e, value), lanes - 1, 1)
        return down, up

    k_w = lane_w % per

    def z_near_packed(packed, own):
        up = pltpu.roll(jnp.where(k_w == W - 1, own, packed), 1, 1)
        down = pltpu.roll(jnp.where(k_w == W, own, packed), lanes - 1, 1)
        return down, up

    def y_near_packed(packed):
        return pltpu.roll(packed, lanes - per, 1), pltpu.roll(packed, per, 1)

    def split(value):
        high = value.astype(bf16)
        low = (value - high.astype(f32)).astype(bf16)
        return jnp.concatenate([high, low], axis=1)

    def split_dot(value, weights):
        return jnp.dot(split(value), weights, preferred_element_type=f32)

    r2 = lax.broadcasted_iota(jnp.int32, (2 * lanes, lanes), 0) % lanes
    c2 = lax.broadcasted_iota(jnp.int32, (2 * lanes, lanes), 1)
    ones = jnp.ones((2 * lanes, lanes), bf16)
    before = jnp.where(r2 < c2, 1.0, jnp.where(r2 == c2, 0.5, 0.0)).astype(bf16)
    both = jnp.concatenate([before, ones], axis=1)
    kr, kc = r2 % per, c2 % per
    same = (r2 // per) == (c2 // per)
    after_w = jnp.where(kr == kc, 0.5, jnp.where((kr >= W) & (kr < kc), 1.0, 0.0))
    before_w = jnp.where(kr == kc, -0.5, jnp.where((kr < W) & (kr > kc), -1.0, 0.0))
    spread_w = jnp.where(same, 1.0, 0.0).astype(bf16)
    packed_sum = jnp.where(same, jnp.where(kc >= W, after_w, before_w), 0.0).astype(bf16)

    zslab = jnp.zeros(perm.shape[1:], f32)
    for ref in (perm, ca, cb, pa, pb):
        ref[0] = zslab
        ref[ny + 1] = zslab
    zrows = jnp.zeros((LO, lanes), f32)

    def clear(y, carry):
        for ref in (perm, pa, pb, ca, cb):
            ref[y + 1, 0:LO, :] = zrows
            ref[y + 1, hi_row:hi_row + LO, :] = zrows
        return carry
    yloop(clear, 0)
    cyp[0] = zslab
    cxp[:, 0:LO, :] = jnp.zeros((ny, LO, lanes), f32)
    hf[...] = jnp.zeros_like(hf)

    for load in loads:
        load.wait()
    zn = jnp.zeros((n, lanes), f32)
    center = pl.ds(mid, n)
    window = pl.ds(LO, wide)

    def own_fields(y, carry):
        zp, zt, zsr, zc = carry
        mark, t, c = m_in[y], t_in[y], c_in[y]
        liq = jnp.where(mark == 1, 1.0, jnp.where(mark == 2, 0.0, f_in[y]))
        solid = 1.0 - liq
        pm = k_in[y] * (liq * liq * liq / (solid * solid + 0.25) + 0.02)
        sr = 2.0 * liq * solid * t
        perm[y + 1, center, :] = pm
        temp[y, center, :] = t
        srcn[y, center, :] = sr
        ca[y + 1, center, :] = c
        rl[y] = SOLUTE_RATE / (liq + 0.1)
        for f, v in enumerate((pm, t, sr)):
            sxs[0, f, y] = v[0:W]
            sxs[1, f, y] = v[n - W:n]
        xs[0, 0, y] = c[0:W]
        xs[0, 1, y] = c[n - W:n]
        hl[y] = split(1.0 + 0.2 * c - 0.3 * t)
        return fold(zp, pm, y), fold(zt, t, y), fold(zsr, sr, y), fold(zc, c, y)

    lane_8 = lax.broadcasted_iota(jnp.int32, (8, lanes), 1)

    def post(s, zc):
        zs[s] = zc
        es[s, 0] = zc[0:W]
        es[s, 1] = zc[n - W:n]
        start(step_copies(s, False))
        sums = jnp.dot(hl[...].reshape(ny * n, 2 * lanes), both, preferred_element_type=f32)
        pf[:, center, :] = sums[:, 0:lanes].reshape(ny, n, lanes)
        totals = sums[:, lanes:2 * lanes].reshape(ny, n, lanes)
        tot = zn
        for y in range(ny):
            tot = jnp.where(lane_n // per == y, totals[y], tot)
        totp[center, :] = tot
        packed = jnp.zeros((8, lanes), f32)
        for j in range(n // 8):
            packed = jnp.where(lane_8 % per == j, tot[8 * j:8 * j + 8], packed)
        ts[s] = packed
        start(step_copies(s, True))

    zp, zt, zsr, zc = yloop(own_fields, (zn,) * 4)
    for f, v in enumerate((zp, zt, zsr)):
        szs[f] = v
        ses[0, f] = v[0:W]
        ses[1, f] = v[n - W:n]
    pl.semaphore_wait(barrier, count)
    start(static_copies())
    post(0, zc)

    top, bottom = pl.ds(LO, W), pl.ds(mid + n, W)
    k_n = lane_n % per
    k_e = lax.broadcasted_iota(jnp.int32, (W, lanes), 1) % per

    arrive(static_copies())
    for f, h in enumerate((PERM, TEMP, SRC)):
        hf[h, center, :] = jnp.where(k_n < W, szr[0, f], szr[1, f])
        hf[h, top, :] = jnp.where(k_e < W, ser[0, 0, f], ser[0, 1, f])
        hf[h, bottom, :] = jnp.where(k_e < W, ser[1, 0, f], ser[1, 1, f])

    def spread(y, carry):
        for f, (ref, o) in enumerate(((perm, 1), (temp, 0), (srcn, 0))):
            ref[y + o, top, :] = sxr[0, f, y]
            ref[y + o, bottom, :] = sxr[1, f, y]
        return carry
    yloop(spread, 0)

    up_rows, down_rows = pl.ds(LO + 1, wide), pl.ds(LO - 1, wide)

    def diagonal_of(pm, near):
        c = [0.5 * (pm + other) for other in near]
        total = c[0] + c[1] + c[2] + c[3] + c[4] + c[5]
        inv = jnp.where(pm > 0.0, 1.0 / jnp.where(pm > 0.0, total, 1.0), 0.0)
        return c, inv

    def coefficients(y, acc):
        pm = perm[y + 1, window, :]
        dz, uz = z_near(pm, hf[PERM, window, :], y)
        c, inv = diagonal_of(pm, [perm[y + 1, up_rows, :], perm[y + 1, down_rows, :],
                                  perm[y + 2, window, :], perm[y, window, :], dz, uz])
        cxp[y, window, :] = c[0]
        cyp[y + 1, window, :] = c[2]

        @pl.when(y == 0)
        def _():
            cyp[0, window, :] = c[3]
        czp[y, window, :] = c[4]
        czm[y, window, :] = c[5]
        for ref, v in zip((axp, axm, ayp, aym, azp, azm), c):
            ref[y] = v * inv
        srcn[y, window, :] = srcn[y, window, :] * inv
        return fold(acc, pm, y)

    zw = jnp.zeros((wide, lanes), f32)
    own = yloop(coefficients, zw)
    pm = hf[PERM, window, :]
    yp, ym = y_near_packed(pm)
    first, last = lane_w < per, lane_w >= lanes - per
    yp, ym = jnp.where(last, 0.0, yp), jnp.where(first, 0.0, ym)
    dz, uz = z_near_packed(pm, own)
    c, inv = diagonal_of(pm, [hf[PERM, up_rows, :], hf[PERM, down_rows, :], yp, ym, dz, uz])
    c[2], c[3] = jnp.where(last, 0.0, c[2]), jnp.where(first, 0.0, c[3])
    for h, v in zip((AXP, AXM, AYP, AYM, AZP, AZM, SRCN), c + [hf[SRC, window, :]]):
        hf[h, window, :] = v * inv

    hx[:, 0:W, :] = sxr[0, 1]
    hx[:, W:2 * W, :] = sxr[1, 1]
    hxt[...] = hx[...]

    conc, conc_next = ca, cb
    for s in range(STEPS):
        arrive(step_copies(s, False))
        hf[CONC, center, :] = jnp.where(k_n < W, zr[s, 0], zr[s, 1])
        hf[CONC, top, :] = jnp.where(k_e < W, er[s, 0, 0], er[s, 0, 1])
        hf[CONC, bottom, :] = jnp.where(k_e < W, er[s, 1, 0], er[s, 1, 1])
        hx[:, 0:W, :] = xr[s, 0]
        hx[:, W:2 * W, :] = xr[s, 1]
        strips = split_dot(1.0 + 0.2 * hx[...].reshape(ny * 2 * W, lanes) - 0.3 * hxt[...].reshape(ny * 2 * W, lanes), both)
        heads = strips[:, 0:lanes].reshape(ny, 2 * W, lanes)
        pf[:, top, :] = heads[:, 0:W]
        pf[:, bottom, :] = heads[:, W:2 * W]
        tails = strips[:, lanes:2 * lanes].reshape(ny, 2 * W, lanes)
        tot = jnp.zeros((2 * W, lanes), f32)
        for y in range(ny):
            tot = jnp.where(lane_8 // per == y, tails[y], tot)
        totp[top, :] = tot[0:W]
        totp[bottom, :] = tot[W:2 * W]
        hpm = hf[PERM, window, :]
        hrho = jnp.where(hpm > 0.0, 1.0 + 0.2 * hf[CONC, window, :] - 0.3 * hf[TEMP, window, :], 0.0)
        hf[RHO, window, :] = hrho

        def head(y, acc, conc=conc, s=s):
            conc[y + 1, top, :] = xr[s, 0, y]
            conc[y + 1, bottom, :] = xr[s, 1, y]
            real = perm[y + 1, window, :] > 0.0
            rho = jnp.where(real, 1.0 + 0.2 * conc[y + 1, window, :] - 0.3 * temp[y, window, :], 0.0)
            pa[y + 1, window, :] = jnp.where(real, gravity * pf[y, window, :], 0.0)
            dz, uz = z_near(rho, hf[RHO, window, :], y)
            down, up = half * (rho + dz), half * (rho + uz)
            ld[y, window, :] = down
            lu[y, window, :] = up
            bb[y] = srcn[y, window, :] - azp[y] * down + azm[y] * up
            return fold(acc, rho, y)

        own = yloop(head, zw)
        arrive(step_copies(s, True))
        total = [tr[s, side, 0] for side in range(3)]
        for d in range(1, nz - 1):
            total = [total[side] + tr[s, side, d] for side in range(3)]
        for j in range(n // 8):
            off[pl.ds(mid + 8 * j, 8), :] = jnp.where(lane_8 % per == j, total[1], 0.0)
        off[top, :] = jnp.where(lane_8 % per == n // 8 - 1, total[0], 0.0)[8 - W:8]
        off[bottom, :] = jnp.where(lane_8 % per == 0, total[2], 0.0)[0:W]
        off[window, :] = split_dot(off[window, :], spread_w)

        def lower(y, carry):
            real = perm[y + 1, window, :] > 0.0
            above = pltpu.roll(off[window, :], lanes - W - y * per, 1)[:, 0:1]
            pa[y + 1, window, :] = pa[y + 1, window, :] + jnp.where(real, gravity * above, 0.0)
            return carry
        yloop(lower, 0)
        above = off[window, :]
        above = jnp.where(k_w >= W, above + totp[window, :], above)
        hf[PH, window, :] = jnp.where(hpm > 0.0, gravity * (above + split_dot(hrho, packed_sum)), 0.0)
        dz, uz = z_near_packed(hrho, own)
        hf[BH, window, :] = hf[SRCN, window, :] - half * (
            hf[AZP, window, :] * (hrho + dz) - hf[AZM, window, :] * (hrho + uz))

        old, new = pa, pb
        for sweep in range(SWEEPS):
            def relax(y, acc, old=old, new=new):
                p = old[y + 1, window, :]
                dz, uz = z_near(p, hf[PH, window, :], y)
                v = bb[y] + axp[y] * old[y + 1, up_rows, :] + axm[y] * old[y + 1, down_rows, :]
                v = v + (ayp[y] * old[y + 2, window, :] + aym[y] * old[y, window, :])
                v = v + (azp[y] * dz + azm[y] * uz)
                new[y + 1, window, :] = v
                return fold(acc, p, y)

            own = yloop(relax, zw)
            p = hf[PH, window, :]
            dz, uz = z_near_packed(p, own)
            yp, ym = y_near_packed(p)
            v = hf[BH, window, :] + hf[AXP, window, :] * hf[PH, up_rows, :] + hf[AXM, window, :] * hf[PH, down_rows, :]
            v = v + hf[AYP, window, :] * yp + hf[AYM, window, :] * ym
            v = v + hf[AZP, window, :] * dz + hf[AZM, window, :] * uz
            hf[PH, window, :] = v
            old, new = new, old

        final = s == STEPS - 1
        up_c, down_c = pl.ds(mid + 1, n), pl.ds(mid - 1, n)

        def transport(y, zc, old=old, conc=conc, conc_next=conc_next, s=s, final=final):
            p, c = old[y + 1, center, :], conc[y + 1, center, :]
            pdz, puz = z_near(p, hf[PH, center, :], y)
            cdz, cuz = z_near(c, hf[CONC, center, :], y)

            def carried(flow, near):
                return flow * jnp.where(flow > 0.0, c, near)

            change = carried(cxp[y, center, :] * (p - old[y + 1, up_c, :]), conc[y + 1, up_c, :])
            change = change + carried(cxp[y, down_c, :] * (p - old[y + 1, down_c, :]), conc[y + 1, down_c, :])
            change = change + carried(cyp[y + 1, center, :] * (p - old[y + 2, center, :]), conc[y + 2, center, :])
            change = change + carried(cyp[y, center, :] * (p - old[y, center, :]), conc[y, center, :])
            change = change + carried(czp[y, center, :] * (p - pdz + ld[y, center, :]), cdz)
            change = change + carried(czm[y, center, :] * (p - puz - lu[y, center, :]), cuz)
            fresh = c - rl[y] * change
            if final:
                p_out[y] = p
                c_out[y] = fresh
                return zc
            conc_next[y + 1, center, :] = fresh
            xs[s + 1, 0, y] = fresh[0:W]
            xs[s + 1, 1, y] = fresh[n - W:n]
            hl[y] = split(1.0 + 0.2 * fresh - 0.3 * t_in[y])
            return fold(zc, fresh, y)

        if final:
            yloop(transport, 0)
        else:
            post(s + 1, yloop(transport, zn))
        conc, conc_next = conc_next, conc

    sent(static_copies())
    for s in range(STEPS):
        sent(step_copies(s, False))
        sent(step_copies(s, True))


def on_device(nx, nz, *args):
    ny, n, lanes = args[0].shape
    wide = n + 2 * W
    rows = wide + 2 * LO
    copies = 2 + 6 + 3 * (nz - 1)

    def vmem(*shape):
        return pltpu.VMEM(shape, jnp.float32)

    padded, layered = (ny + 2, rows, lanes), (ny, rows, lanes)
    scratch = [pltpu.VMEM((ny, n, lanes), a.dtype) for a in args]
    scratch += [vmem(*padded), vmem(*layered)] + [vmem(*padded)] * 4
    scratch += [vmem(ny, wide, lanes)] * 6 + [vmem(*layered)]
    scratch += [vmem(*layered), vmem(ny + 1, rows, lanes), vmem(*layered), vmem(*layered),
                vmem(ny, n, lanes), vmem(ny, wide, lanes), vmem(*layered), vmem(*layered)]
    scratch += [vmem(14, rows, lanes), vmem(rows, lanes), vmem(rows, lanes)]
    scratch += [pltpu.VMEM((ny, n, 2 * lanes), jnp.bfloat16), vmem(*layered)] + [vmem(ny, 2 * W, lanes)] * 2
    scratch += [vmem(STEPS, 2, ny, W, lanes)] * 2
    scratch += [vmem(STEPS, n, lanes), vmem(STEPS, 2, n, lanes)]
    scratch += [vmem(STEPS, 2, W, lanes), vmem(STEPS, 2, 2, W, lanes)]
    scratch += [vmem(STEPS, 8, lanes), vmem(STEPS, 3, nz - 1, 8, lanes)]
    scratch += [vmem(2, 3, ny, W, lanes)] * 2
    scratch += [vmem(3, n, lanes), vmem(2, 3, n, lanes), vmem(2, 3, W, lanes), vmem(2, 2, 3, W, lanes)]
    scratch += [pltpu.SemaphoreType.DMA((STEPS, copies))] * 2 + [pltpu.SemaphoreType.DMA((8,))] * 2
    scratch += [pltpu.SemaphoreType.DMA((5,))]
    return tuple(pl.pallas_call(
        functools.partial(kernel, nx, nz),
        out_shape=[jax.ShapeDtypeStruct((ny, n, lanes), jnp.float32)] * 2,
        in_specs=[pl.BlockSpec(memory_space=pltpu.HBM)] * 5,
        out_specs=[pl.BlockSpec(memory_space=pltpu.VMEM)] * 2,
        scratch_shapes=scratch,
        compiler_params=pltpu.CompilerParams(
            collective_id=0, has_side_effects=True, vmem_limit_bytes=63 * 1024 * 1024),
    )(*args))


def solution(mesh):
    placed = P(None, "gx", "gz")
    return jax.shard_map(
        functools.partial(on_device, mesh.shape["gx"], mesh.shape["gz"]),
        mesh=mesh,
        in_specs=(placed,) * 5,
        out_specs=(placed, placed),
        check_vma=False,
    )
```

```python
import functools

import jax
import jax.numpy as jnp
from jax import lax
from jax.experimental import pallas as pl
from jax.experimental.pallas import tpu as pltpu
from jax.sharding import PartitionSpec as P

STEPS = 4
SWEEPS = 3
W = SWEEPS + 1
SOLUTE_RATE = 0.5
MESH = pl.DeviceIdType.MESH
UNROLL = 4

LO = 8


def kernel(nx, nz, *refs):
    it = iter(refs)
    hbm = [next(it) for _ in range(5)]
    p_out, c_out = [next(it) for _ in range(2)]
    t_in, c_in, f_in, k_in, m_in = staged = [next(it) for _ in range(5)]
    perm, temp, ca, cb, pa, pb = [next(it) for _ in range(6)]
    axp, axm, ayp, aym, azp, azm, srcn = [next(it) for _ in range(7)]
    cxp, cyp, czp, czm, rl, bb, ld, lu = [next(it) for _ in range(8)]
    hf = next(it)
    off, totp, hl, pf, hx, hxt = [next(it) for _ in range(6)]
    xs, xr, zs, zr, es, er, ts, tr = [next(it) for _ in range(8)]
    sxs, sxr, szs, szr, ses, ser = [next(it) for _ in range(6)]
    send_sem, recv_sem, st_send, st_recv, in_sem = [next(it) for _ in range(5)]

    ny, n, lanes = t_in.shape
    wide = n + 2 * W
    hi_row = LO + wide
    mid = LO + W
    gravity = 4.0 / (nz * lanes)
    half = 0.5 * gravity
    ix, iz = lax.axis_index("gx"), lax.axis_index("gz")
    f32, bf16 = jnp.float32, jnp.bfloat16

    CONC, PERM, TEMP, SRC, PH, BH, AXP, AXM, AYP, AYM, AZP, AZM, SRCN, RHO = range(14)

    def inside(dx, dz):
        return (ix + dx >= 0) & (ix + dx < nx) & (iz + dz >= 0) & (iz + dz < nz)

    partners = [(dx, dz) for dz in range(-1, nz) for dx in (-1, 0, 1) if (dx, dz) != (0, 0)]

    def step_copies(s, totals):
        plan = []
        for dx, dz in partners:
            a, b = (1, 0) if dx > 0 else (0, 1)
            if dz == 0:
                plan.append((dx, dz, xs.at[s, a], xr.at[s, b]))
            elif dz in (-1, 1) and dx == 0:
                plan.append((dx, dz, zs.at[s], zr.at[s, 0 if dz > 0 else 1]))
            elif dz in (-1, 1):
                plan.append((dx, dz, es.at[s, a], er.at[s, b, 0 if dz > 0 else 1]))
            if dz > 0:
                plan.append((dx, dz, ts.at[s], tr.at[s, 1 - dx, dz - 1]))
        return [(dx, dz, pltpu.make_async_remote_copy(
            src_ref=src, dst_ref=dst, send_sem=send_sem.at[s, m], recv_sem=recv_sem.at[s, m],
            device_id={"gx": ix + dx, "gz": iz + dz}, device_id_type=MESH))
            for m, (dx, dz, src, dst) in enumerate(plan) if (dst.shape == (8, lanes)) == totals]

    def static_copies():
        out = []
        for dx, dz in partners:
            if dz > 1:
                continue
            a, b = (1, 0) if dx > 0 else (0, 1)
            if dz == 0:
                src, dst = sxs.at[a], sxr.at[b]
            elif dx == 0:
                src, dst = szs, szr.at[0 if dz > 0 else 1]
            else:
                src, dst = ses.at[a], ser.at[b, 0 if dz > 0 else 1]
            m = len(out)
            out.append((dx, dz, pltpu.make_async_remote_copy(
                src_ref=src, dst_ref=dst, send_sem=st_send.at[m], recv_sem=st_recv.at[m],
                device_id={"gx": ix + dx, "gz": iz + dz}, device_id_type=MESH)))
        return out

    def start(copies):
        for dx, dz, c in copies:
            pl.when(inside(dx, dz))(c.start)

    def arrive(copies):
        for dx, dz, c in copies:
            pl.when(inside(-dx, -dz))(c.wait_recv)

    def sent(copies):
        for dx, dz, c in copies:
            pl.when(inside(dx, dz))(c.wait_send)

    loads = [pltpu.make_async_copy(a, b, in_sem.at[i]) for i, (a, b) in enumerate(zip(hbm, staged))]
    for load in loads:
        load.start()

    for ref in (xr, zr, er, tr, sxr, szr, ser):
        ref[...] = jnp.zeros_like(ref)
    barrier = pltpu.get_barrier_semaphore()
    count = 0
    for dx, dz in partners:
        @pl.when(inside(-dx, -dz))
        def _(dx=dx, dz=dz):
            pl.semaphore_signal(barrier, inc=1, device_id={"gx": ix - dx, "gz": iz - dz}, device_id_type=MESH)
        count = count + inside(dx, dz).astype(jnp.int32)

    def yloop(body, init, unroll=UNROLL):
        def group(g, carry):
            for u in range(unroll):
                carry = body(g * unroll + u, carry)
            return carry
        return lax.fori_loop(0, ny // unroll, group, init)

    lane_n = lax.broadcasted_iota(jnp.int32, (n, lanes), 1)
    lane_w = lax.broadcasted_iota(jnp.int32, (wide, lanes), 1)
    per = lanes // ny

    def lane(rows):
        return lane_n if rows == n else lane_w

    def fold(acc, value, y, roll=True):
        moved = pltpu.roll(value, y * per + W, 1) if roll else value
        return jnp.where(lane(value.shape[0]) // per == y, moved, acc)

    def z_near(value, packed, y):
        e = pltpu.roll(packed, lanes - W - y * per, 1)
        ln = lane(value.shape[0])
        up = pltpu.roll(jnp.where(ln == lanes - 1, e, value), 1, 1)
        down = pltpu.roll(jnp.where(ln == 0, e, value), lanes - 1, 1)
        return down, up

    k_w = lane_w % per

    def z_near_packed(packed, own):
        up = pltpu.roll(jnp.where(k_w == W - 1, own, packed), 1, 1)
        down = pltpu.roll(jnp.where(k_w == W, own, packed), lanes - 1, 1)
        return down, up

    def y_near_packed(packed):
        return pltpu.roll(packed, lanes - per, 1), pltpu.roll(packed, per, 1)

    def split(value):
        high = value.astype(bf16)
        low = (value - high.astype(f32)).astype(bf16)
        return jnp.concatenate([high, low], axis=1)

    def split_dot(value, weights):
        return jnp.dot(split(value), weights, preferred_element_type=f32)

    r2 = lax.broadcasted_iota(jnp.int32, (2 * lanes, lanes), 0) % lanes
    c2 = lax.broadcasted_iota(jnp.int32, (2 * lanes, lanes), 1)
    ones = jnp.ones((2 * lanes, lanes), bf16)
    before = jnp.where(r2 < c2, 1.0, jnp.where(r2 == c2, 0.5, 0.0)).astype(bf16)
    both = jnp.concatenate([before, ones], axis=1)
    kr, kc = r2 % per, c2 % per
    same = (r2 // per) == (c2 // per)
    after_w = jnp.where(kr == kc, 0.5, jnp.where((kr >= W) & (kr < kc), 1.0, 0.0))
    before_w = jnp.where(kr == kc, -0.5, jnp.where((kr < W) & (kr > kc), -1.0, 0.0))
    spread_w = jnp.where(same, 1.0, 0.0).astype(bf16)
    packed_sum = jnp.where(same, jnp.where(kc >= W, after_w, before_w), 0.0).astype(bf16)

    zslab = jnp.zeros(perm.shape[1:], f32)
    for ref in (perm, ca, cb, pa, pb):
        ref[0] = zslab
        ref[ny + 1] = zslab
    zrows = jnp.zeros((LO, lanes), f32)

    def clear(y, carry):
        for ref in (perm, pa, pb, ca, cb):
            ref[y + 1, 0:LO, :] = zrows
            ref[y + 1, hi_row:hi_row + LO, :] = zrows
        return carry
    yloop(clear, 0)
    cyp[0] = zslab
    cxp[:, 0:LO, :] = jnp.zeros((ny, LO, lanes), f32)
    hf[...] = jnp.zeros_like(hf)

    for load in loads:
        load.wait()
    zn = jnp.zeros((n, lanes), f32)
    center = pl.ds(mid, n)
    window = pl.ds(LO, wide)

    def own_fields(y, carry):
        zp, zt, zsr, zc = carry
        mark, t, c = m_in[y], t_in[y], c_in[y]
        liq = jnp.where(mark == 1, 1.0, jnp.where(mark == 2, 0.0, f_in[y]))
        solid = 1.0 - liq
        pm = k_in[y] * (liq * liq * liq / (solid * solid + 0.25) + 0.02)
        sr = 2.0 * liq * solid * t
        perm[y + 1, center, :] = pm
        temp[y, center, :] = t
        srcn[y, center, :] = sr
        ca[y + 1, center, :] = c
        rl[y] = SOLUTE_RATE / (liq + 0.1)
        for f, v in enumerate((pm, t, sr)):
            sxs[0, f, y] = v[0:W]
            sxs[1, f, y] = v[n - W:n]
        xs[0, 0, y] = c[0:W]
        xs[0, 1, y] = c[n - W:n]
        hl[y] = split(1.0 + 0.2 * c - 0.3 * t)
        return fold(zp, pm, y), fold(zt, t, y), fold(zsr, sr, y), fold(zc, c, y)

    lane_8 = lax.broadcasted_iota(jnp.int32, (8, lanes), 1)

    def post(s, zc):
        zs[s] = zc
        es[s, 0] = zc[0:W]
        es[s, 1] = zc[n - W:n]
        start(step_copies(s, False))
        sums = jnp.dot(hl[...].reshape(ny * n, 2 * lanes), both, preferred_element_type=f32)
        pf[:, center, :] = sums[:, 0:lanes].reshape(ny, n, lanes)
        totals = sums[:, lanes:2 * lanes].reshape(ny, n, lanes)
        tot = zn
        for y in range(ny):
            tot = jnp.where(lane_n // per == y, totals[y], tot)
        totp[center, :] = tot
        packed = jnp.zeros((8, lanes), f32)
        for j in range(n // 8):
            packed = jnp.where(lane_8 % per == j, tot[8 * j:8 * j + 8], packed)
        ts[s] = packed
        start(step_copies(s, True))

    zp, zt, zsr, zc = yloop(own_fields, (zn,) * 4)
    for f, v in enumerate((zp, zt, zsr)):
        szs[f] = v
        ses[0, f] = v[0:W]
        ses[1, f] = v[n - W:n]
    pl.semaphore_wait(barrier, count)
    start(static_copies())
    post(0, zc)

    top, bottom = pl.ds(LO, W), pl.ds(mid + n, W)
    k_n = lane_n % per
    k_e = lax.broadcasted_iota(jnp.int32, (W, lanes), 1) % per

    arrive(static_copies())
    for f, h in enumerate((PERM, TEMP, SRC)):
        hf[h, center, :] = jnp.where(k_n < W, szr[0, f], szr[1, f])
        hf[h, top, :] = jnp.where(k_e < W, ser[0, 0, f], ser[0, 1, f])
        hf[h, bottom, :] = jnp.where(k_e < W, ser[1, 0, f], ser[1, 1, f])

    def spread(y, carry):
        for f, (ref, o) in enumerate(((perm, 1), (temp, 0), (srcn, 0))):
            ref[y + o, top, :] = sxr[0, f, y]
            ref[y + o, bottom, :] = sxr[1, f, y]
        return carry
    yloop(spread, 0)

    up_rows, down_rows = pl.ds(LO + 1, wide), pl.ds(LO - 1, wide)

    def diagonal_of(pm, near):
        c = [0.5 * (pm + other) for other in near]
        total = c[0] + c[1] + c[2] + c[3] + c[4] + c[5]
        inv = jnp.where(pm > 0.0, 1.0 / jnp.where(pm > 0.0, total, 1.0), 0.0)
        return c, inv

    def coefficients(y, acc):
        pm = perm[y + 1, window, :]
        dz, uz = z_near(pm, hf[PERM, window, :], y)
        c, inv = diagonal_of(pm, [perm[y + 1, up_rows, :], perm[y + 1, down_rows, :],
                                  perm[y + 2, window, :], perm[y, window, :], dz, uz])
        cxp[y, window, :] = c[0]
        cyp[y + 1, window, :] = c[2]

        @pl.when(y == 0)
        def _():
            cyp[0, window, :] = c[3]
        czp[y, window, :] = c[4]
        czm[y, window, :] = c[5]
        for ref, v in zip((axp, axm, ayp, aym, azp, azm), c):
            ref[y] = v * inv
        srcn[y, window, :] = srcn[y, window, :] * inv
        return fold(acc, pm, y)

    zw = jnp.zeros((wide, lanes), f32)
    own = yloop(coefficients, zw)
    pm = hf[PERM, window, :]
    yp, ym = y_near_packed(pm)
    first, last = lane_w < per, lane_w >= lanes - per
    yp, ym = jnp.where(last, 0.0, yp), jnp.where(first, 0.0, ym)
    dz, uz = z_near_packed(pm, own)
    c, inv = diagonal_of(pm, [hf[PERM, up_rows, :], hf[PERM, down_rows, :], yp, ym, dz, uz])
    c[2], c[3] = jnp.where(last, 0.0, c[2]), jnp.where(first, 0.0, c[3])
    for h, v in zip((AXP, AXM, AYP, AYM, AZP, AZM, SRCN), c + [hf[SRC, window, :]]):
        hf[h, window, :] = v * inv

    hx[:, 0:W, :] = sxr[0, 1]
    hx[:, W:2 * W, :] = sxr[1, 1]
    hxt[...] = hx[...]

    conc, conc_next = ca, cb
    for s in range(STEPS):
        arrive(step_copies(s, False))
        hf[CONC, center, :] = jnp.where(k_n < W, zr[s, 0], zr[s, 1])
        hf[CONC, top, :] = jnp.where(k_e < W, er[s, 0, 0], er[s, 0, 1])
        hf[CONC, bottom, :] = jnp.where(k_e < W, er[s, 1, 0], er[s, 1, 1])
        hx[:, 0:W, :] = xr[s, 0]
        hx[:, W:2 * W, :] = xr[s, 1]
        strips = split_dot(1.0 + 0.2 * hx[...].reshape(ny * 2 * W, lanes) - 0.3 * hxt[...].reshape(ny * 2 * W, lanes), both)
        heads = strips[:, 0:lanes].reshape(ny, 2 * W, lanes)
        pf[:, top, :] = heads[:, 0:W]
        pf[:, bottom, :] = heads[:, W:2 * W]
        tails = strips[:, lanes:2 * lanes].reshape(ny, 2 * W, lanes)
        tot = jnp.zeros((2 * W, lanes), f32)
        for y in range(ny):
            tot = jnp.where(lane_8 // per == y, tails[y], tot)
        totp[top, :] = tot[0:W]
        totp[bottom, :] = tot[W:2 * W]
        hpm = hf[PERM, window, :]
        hrho = jnp.where(hpm > 0.0, 1.0 + 0.2 * hf[CONC, window, :] - 0.3 * hf[TEMP, window, :], 0.0)
        hf[RHO, window, :] = hrho

        def head(y, acc, conc=conc, s=s):
            conc[y + 1, top, :] = xr[s, 0, y]
            conc[y + 1, bottom, :] = xr[s, 1, y]
            real = perm[y + 1, window, :] > 0.0
            rho = jnp.where(real, 1.0 + 0.2 * conc[y + 1, window, :] - 0.3 * temp[y, window, :], 0.0)
            pa[y + 1, window, :] = jnp.where(real, gravity * pf[y, window, :], 0.0)
            dz, uz = z_near(rho, hf[RHO, window, :], y)
            down, up = half * (rho + dz), half * (rho + uz)
            ld[y, window, :] = down
            lu[y, window, :] = up
            bb[y] = srcn[y, window, :] - azp[y] * down + azm[y] * up
            return fold(acc, rho, y)

        own = yloop(head, zw)
        arrive(step_copies(s, True))
        total = [tr[s, side, 0] for side in range(3)]
        for d in range(1, nz - 1):
            total = [total[side] + tr[s, side, d] for side in range(3)]
        for j in range(n // 8):
            off[pl.ds(mid + 8 * j, 8), :] = jnp.where(lane_8 % per == j, total[1], 0.0)
        off[top, :] = jnp.where(lane_8 % per == n // 8 - 1, total[0], 0.0)[8 - W:8]
        off[bottom, :] = jnp.where(lane_8 % per == 0, total[2], 0.0)[0:W]
        off[window, :] = split_dot(off[window, :], spread_w)

        def lower(y, carry):
            real = perm[y + 1, window, :] > 0.0
            above = pltpu.roll(off[window, :], lanes - W - y * per, 1)[:, 0:1]
            pa[y + 1, window, :] = pa[y + 1, window, :] + jnp.where(real, gravity * above, 0.0)
            return carry
        yloop(lower, 0)
        above = off[window, :]
        above = jnp.where(k_w >= W, above + totp[window, :], above)
        hf[PH, window, :] = jnp.where(hpm > 0.0, gravity * (above + split_dot(hrho, packed_sum)), 0.0)
        dz, uz = z_near_packed(hrho, own)
        hf[BH, window, :] = hf[SRCN, window, :] - half * (
            hf[AZP, window, :] * (hrho + dz) - hf[AZM, window, :] * (hrho + uz))

        old, new = pa, pb
        for sweep in range(SWEEPS):
            def relax(y, acc, old=old, new=new):
                p = old[y + 1, window, :]
                dz, uz = z_near(p, hf[PH, window, :], y)
                v = bb[y] + axp[y] * old[y + 1, up_rows, :] + axm[y] * old[y + 1, down_rows, :]
                v = v + (ayp[y] * old[y + 2, window, :] + aym[y] * old[y, window, :])
                v = v + (azp[y] * dz + azm[y] * uz)
                new[y + 1, window, :] = v
                return fold(acc, p, y)

            own = yloop(relax, zw, 8)
            p = hf[PH, window, :]
            dz, uz = z_near_packed(p, own)
            yp, ym = y_near_packed(p)
            v = hf[BH, window, :] + hf[AXP, window, :] * hf[PH, up_rows, :] + hf[AXM, window, :] * hf[PH, down_rows, :]
            v = v + hf[AYP, window, :] * yp + hf[AYM, window, :] * ym
            v = v + hf[AZP, window, :] * dz + hf[AZM, window, :] * uz
            hf[PH, window, :] = v
            old, new = new, old

        final = s == STEPS - 1
        up_c, down_c = pl.ds(mid + 1, n), pl.ds(mid - 1, n)

        def transport(y, zc, old=old, conc=conc, conc_next=conc_next, s=s, final=final):
            p, c = old[y + 1, center, :], conc[y + 1, center, :]
            pdz, puz = z_near(p, hf[PH, center, :], y)
            cdz, cuz = z_near(c, hf[CONC, center, :], y)

            def carried(flow, near):
                return flow * jnp.where(flow > 0.0, c, near)

            change = carried(cxp[y, center, :] * (p - old[y + 1, up_c, :]), conc[y + 1, up_c, :])
            change = change + carried(cxp[y, down_c, :] * (p - old[y + 1, down_c, :]), conc[y + 1, down_c, :])
            change = change + carried(cyp[y + 1, center, :] * (p - old[y + 2, center, :]), conc[y + 2, center, :])
            change = change + carried(cyp[y, center, :] * (p - old[y, center, :]), conc[y, center, :])
            change = change + carried(czp[y, center, :] * (p - pdz + ld[y, center, :]), cdz)
            change = change + carried(czm[y, center, :] * (p - puz - lu[y, center, :]), cuz)
            fresh = c - rl[y] * change
            if final:
                p_out[y] = p
                c_out[y] = fresh
                return zc
            conc_next[y + 1, center, :] = fresh
            xs[s + 1, 0, y] = fresh[0:W]
            xs[s + 1, 1, y] = fresh[n - W:n]
            hl[y] = split(1.0 + 0.2 * fresh - 0.3 * t_in[y])
            return fold(zc, fresh, y)

        if final:
            yloop(transport, 0)
        else:
            post(s + 1, yloop(transport, zn))
        conc, conc_next = conc_next, conc

    sent(static_copies())
    for s in range(STEPS):
        sent(step_copies(s, False))
        sent(step_copies(s, True))


def on_device(nx, nz, *args):
    ny, n, lanes = args[0].shape
    wide = n + 2 * W
    rows = wide + 2 * LO
    copies = 2 + 6 + 3 * (nz - 1)

    def vmem(*shape):
        return pltpu.VMEM(shape, jnp.float32)

    padded, layered = (ny + 2, rows, lanes), (ny, rows, lanes)
    scratch = [pltpu.VMEM((ny, n, lanes), a.dtype) for a in args]
    scratch += [vmem(*padded), vmem(*layered)] + [vmem(*padded)] * 4
    scratch += [vmem(ny, wide, lanes)] * 6 + [vmem(*layered)]
    scratch += [vmem(*layered), vmem(ny + 1, rows, lanes), vmem(*layered), vmem(*layered),
                vmem(ny, n, lanes), vmem(ny, wide, lanes), vmem(*layered), vmem(*layered)]
    scratch += [vmem(14, rows, lanes), vmem(rows, lanes), vmem(rows, lanes)]
    scratch += [pltpu.VMEM((ny, n, 2 * lanes), jnp.bfloat16), vmem(*layered)] + [vmem(ny, 2 * W, lanes)] * 2
    scratch += [vmem(STEPS, 2, ny, W, lanes)] * 2
    scratch += [vmem(STEPS, n, lanes), vmem(STEPS, 2, n, lanes)]
    scratch += [vmem(STEPS, 2, W, lanes), vmem(STEPS, 2, 2, W, lanes)]
    scratch += [vmem(STEPS, 8, lanes), vmem(STEPS, 3, nz - 1, 8, lanes)]
    scratch += [vmem(2, 3, ny, W, lanes)] * 2
    scratch += [vmem(3, n, lanes), vmem(2, 3, n, lanes), vmem(2, 3, W, lanes), vmem(2, 2, 3, W, lanes)]
    scratch += [pltpu.SemaphoreType.DMA((STEPS, copies))] * 2 + [pltpu.SemaphoreType.DMA((8,))] * 2
    scratch += [pltpu.SemaphoreType.DMA((5,))]
    return tuple(pl.pallas_call(
        functools.partial(kernel, nx, nz),
        out_shape=[jax.ShapeDtypeStruct((ny, n, lanes), jnp.float32)] * 2,
        in_specs=[pl.BlockSpec(memory_space=pltpu.HBM)] * 5,
        out_specs=[pl.BlockSpec(memory_space=pltpu.VMEM)] * 2,
        scratch_shapes=scratch,
        compiler_params=pltpu.CompilerParams(
            collective_id=0, has_side_effects=True, vmem_limit_bytes=63 * 1024 * 1024),
    )(*args))


def solution(mesh):
    placed = P(None, "gx", "gz")
    return jax.shard_map(
        functools.partial(on_device, mesh.shape["gx"], mesh.shape["gz"]),
        mesh=mesh,
        in_specs=(placed,) * 5,
        out_specs=(placed, placed),
        check_vma=False,
    )
```
